32 devices in a mesh: tok: 4 (over z), head: 4 (over y, x), grp: 2 (over core).
Axes of the slice: x: 2, y: 2, z: 4, core: 2. Of those that a mesh axis runs over, the one named last changes fastest.
Arguments:
- tokens: bfloat16 [2048, 4096], P('tok', ('head', 'grp')), may hold values from -6 to 6
- norm_gain: bfloat16 [4096], P(('head', 'grp')), may hold values from 1.2 to 9, as said below
- query_key_value_weight: bfloat16 [4096, 6144], P(None, ('head', 'grp')), may hold values from -0.09375 to 0.09375
- out_weight: bfloat16 [4096, 4096], P(('head', 'grp')), may hold values from -0.09375 to 0.09375
- doc_ids: int32 [2048], P('tok'), may hold values from 0 to 3, never falling along the last dimension, each value on 1 to 1024 neighbouring positions
Outputs:
- attended: bfloat16 [2048, 4096], P('tok', ('head', 'grp'))
The draws below stay inside these ranges and needn't reach their ends.
Inputs may be any that keep to these rules, and one draw needn't show every extreme that they name: `norm_gain`: norm gains are positive. `doc_ids`: non-decreasing along the window; each document has 1 to 1024 tokens and one has exactly 1024.
All inputs are finite; a program needn't handle non-finite values.
Results may differ from the reference program's by a relative error of at most 0.019.
The reference program's roundings to bfloat16 on the way count: a program that leaves them out, or rounds other values in their place, can miss the bound.
Values may be sent and summed in bfloat16 or wider, within the bound.
A program may use at most 128 MiB of HBM per device.

```python
import math
import jax
import jax.numpy as jnp
import numpy as np
from jax import lax

MODEL_WIDTH = 4096
QUERY_HEADS = 32
KEY_VALUE_HEADS = 8
HEAD_SIZE = 128
WINDOW_TOKENS = 2048
DOC_MOST = 1024
DOC_COUNT = 4


def draw_norm_gain(key, part):
    gains = jax.random.uniform(key, (MODEL_WIDTH,), jnp.float32, 1.2, 2.2)
    return gains.astype(jnp.bfloat16)


def shard_levels(key, shape, split, smallest, high):
    factor_of = 1.0
    for dim, parts in split:
        steps = jax.random.uniform(jax.random.fold_in(jax.random.fold_in(key, 6), dim), (parts,), jnp.float32, smallest / len(split), high / len(split))
        factor_of = factor_of * jnp.repeat(jnp.exp(steps), shape[dim] // parts).reshape((-1,) + (1,) * (len(shape) - 1 - dim))
    return factor_of


def profile(count, total, limit, slope):
    portions = [(1 << 20) // math.isqrt(grade ** slope) + 1 for grade in range(2, count + 1)]
    rest, holding = total - limit - (count - 1), [1] * (count - 1)
    while rest > 0:
        movable = [i for i in range(count - 1) if holding[i] < limit]
        pool, budget = sum([portions[i] for i in movable]), rest
        for i in movable:
            more = min(limit - holding[i], max(1, budget * portions[i] // pool), rest)
            holding[i] = holding[i] + more
            rest = rest - more
    return np.array([limit] + holding)


def ragged_sizes(key, number_of, total, most, slope):
    if number_of == 2:
        one = jax.random.randint(key, (), max(1, total - most), min(most, total - 1) + 1)
        return jnp.stack([one, total - one])
    lengths = jnp.asarray(profile(number_of, total, most, slope), jnp.int32)
    couples = (number_of - 1) // 2
    giver, receiver = lengths[1:1 + 2 * couples:2], lengths[2:2 + 2 * couples:2]
    margin = jnp.minimum(giver - 1, most - receiver)
    passed = jax.random.randint(jax.random.fold_in(key, 1), (couples,), 0, 1 << 20) % (margin + 1)
    lengths = lengths.at[1:1 + 2 * couples:2].set(giver - passed).at[2:2 + 2 * couples:2].set(receiver + passed)
    return lengths[jax.random.permutation(jax.random.fold_in(key, 2), number_of)]


def bell_draw(own_key, dims, width, bound, cuts=(), held_as=jnp.bfloat16):
    loudness = shard_levels(own_key, dims, cuts, -0.22, 0.18) if cuts else 1.0
    drawn = jax.random.normal(own_key, dims, jnp.float32) * width * loudness
    return jnp.minimum(jnp.maximum(drawn, -bound), bound).astype(held_as)


def setup_inputs(seed: int = 0) -> dict:
    streams_of = jax.random.split(jax.random.key(seed), 6)
    return {
        "tokens": bell_draw(streams_of[0], (WINDOW_TOKENS, MODEL_WIDTH), 1.0, 6.0, ((0, 4), (1, 8))),
        "norm_gain": draw_norm_gain(jax.random.fold_in(streams_of[5], 71), 0),
        "query_key_value_weight": bell_draw(streams_of[2], (MODEL_WIDTH, (QUERY_HEADS + 2 * KEY_VALUE_HEADS) * HEAD_SIZE), MODEL_WIDTH ** -0.5, 0.09375, ((1, 8),)),
        "out_weight": bell_draw(streams_of[3], (QUERY_HEADS * HEAD_SIZE, MODEL_WIDTH), (QUERY_HEADS * HEAD_SIZE) ** -0.5, 0.09375, ((0, 8),)),
        "doc_ids": jnp.searchsorted(jnp.cumsum(ragged_sizes(streams_of[4], DOC_COUNT, WINDOW_TOKENS, DOC_MOST, 2)), jnp.arange(WINDOW_TOKENS), side="right").astype(jnp.int32),
    }


epsilon = 1e-05
theta = 500000.0

def rotate(vectors, positions):
    half = vectors.shape[-1] // 2
    inverse = 1.0 / theta ** (jnp.arange(half, dtype=jnp.float32) * (2.0 / vectors.shape[-1]))
    angles = positions.astype(jnp.float32)[:, None] * inverse[None, :]
    cosine = jnp.cos(angles)[:, None, :]
    sine = jnp.sin(angles)[:, None, :]
    first = vectors[..., :half]
    second = vectors[..., half:]
    return jnp.concatenate([first * cosine - second * sine, second * cosine + first * sine], axis=-1)

def reference(tokens, norm_gain, query_key_value_weight, out_weight, doc_ids):
    head_group = QUERY_HEADS // KEY_VALUE_HEADS
    floats = tokens.astype(jnp.float32)
    normed_input = (floats * lax.rsqrt(lax.optimization_barrier(jnp.mean(floats * floats, axis=1, keepdims=True)) + epsilon) * norm_gain.astype(jnp.float32)).astype(jnp.bfloat16)
    mixed_output = jnp.dot(normed_input, query_key_value_weight, preferred_element_type=jnp.float32).reshape(WINDOW_TOKENS, KEY_VALUE_HEADS, (head_group + 2) * HEAD_SIZE)
    positions = jnp.arange(WINDOW_TOKENS, dtype=jnp.int32)
    query_rows = rotate(mixed_output[:, :, :head_group * HEAD_SIZE].reshape(WINDOW_TOKENS, QUERY_HEADS, HEAD_SIZE), positions).astype(jnp.bfloat16)
    keys = rotate(mixed_output[:, :, head_group * HEAD_SIZE:(head_group + 1) * HEAD_SIZE], positions).astype(jnp.bfloat16)
    values = mixed_output[:, :, (head_group + 1) * HEAD_SIZE:].astype(jnp.bfloat16)
    tile_block = 512 if WINDOW_TOKENS % 512 == 0 else WINDOW_TOKENS
    window = min(WINDOW_TOKENS, DOC_MOST + tile_block)
    scale = HEAD_SIZE ** (-0.5)

    def attend(index):
        query_begin = (index * tile_block).astype(jnp.int32)
        key_start = jnp.clip(query_begin + tile_block - window, 0, WINDOW_TOKENS - window).astype(jnp.int32)
        query_portion = lax.dynamic_slice_in_dim(query_rows, query_begin, tile_block, 0).reshape(tile_block, KEY_VALUE_HEADS, head_group, HEAD_SIZE).astype(jnp.float32)
        key_part = lax.dynamic_slice_in_dim(keys, key_start, window, 0).astype(jnp.float32)
        value_part = lax.dynamic_slice_in_dim(values, key_start, window, 0).astype(jnp.float32)
        query_docs = lax.dynamic_slice_in_dim(doc_ids, query_begin, tile_block, 0)
        key_docs = lax.dynamic_slice_in_dim(doc_ids, key_start, window, 0)
        query_positions = query_begin + jnp.arange(tile_block, dtype=jnp.int32)
        key_positions = key_start + jnp.arange(window, dtype=jnp.int32)
        mask = (key_positions[None, :] <= query_positions[:, None]) & (key_docs[None, :] == query_docs[:, None])
        scores = jnp.einsum('qgjd,kgd->gjqk', query_portion, key_part) * scale
        highest = lax.optimization_barrier(jnp.max(jnp.where(mask, scores, -1e+30), axis=-1, keepdims=True))
        weights = jnp.where(mask, jnp.exp(scores - highest), 0.0)
        totals = lax.optimization_barrier(jnp.sum(weights, axis=-1))
        rounded = lax.optimization_barrier(weights.astype(jnp.bfloat16)).astype(jnp.float32)
        summed = jnp.einsum('gjqk,kgd->qgjd', rounded, value_part)
        normal = summed / jnp.transpose(totals, (2, 0, 1))[..., None]
        return normal.astype(jnp.bfloat16).reshape(tile_block, QUERY_HEADS * HEAD_SIZE)
    heads = lax.map(attend, jnp.arange(WINDOW_TOKENS // tile_block, dtype=jnp.int32)).reshape(WINDOW_TOKENS, QUERY_HEADS * HEAD_SIZE)
    return jnp.dot(heads, out_weight, preferred_element_type=jnp.float32).astype(jnp.bfloat16)
```

```python
import functools

import jax
import jax.numpy as jnp
import numpy as np
from jax import lax
from jax.experimental import pallas as pl
from jax.experimental.pallas import tpu as pltpu
from jax.sharding import PartitionSpec as P

QUERY_HEADS = 32
KEY_VALUE_HEADS = 8
HEAD_SIZE = 128
GROUP = QUERY_HEADS // KEY_VALUE_HEADS

epsilon = 1e-05
theta = 500000.0
floor_score = -1e30
HEADER = 16
CHUNKS = 4
MESH = pl.DeviceIdType.MESH


def kernel(
    size, tokens_hbm, gain_ref, wqkv_hbm, wout_hbm, docs_ref, local_ref, base_ref, out_ref,
    gath, wqkv, wout, queries, kvs, mixed, owners, highs, totals, accums,
    sib_out, sib_in, part, x_out, x_in,
    load_sem, ag_send, ag_recv, kv_send, kv_recv, sib_send, sib_recv, x_send, x_recv,
):
    tok_size, reach = size, size // 2
    length, width = tokens_hbm.shape
    blocks = gath.shape[0]
    chips = blocks // 2
    rows = length // CHUNKS
    t = lax.axis_index("tok")
    h = lax.axis_index("head")
    c = lax.axis_index("grp")
    hx = h + 1 - 2 * (h % 2)
    hy = h + 2 - 4 * ((h // 2) % 2)
    ha = hx * (1 - c) + hy * c
    hb = hy * (1 - c) + hx * c
    hd = hx + hy - h
    s = 1 - c
    me = h * 2 + c
    to_a, to_b, to_sib = {"head": ha}, {"head": hb}, {"grp": s}

    load_tokens = pltpu.make_async_copy(
        tokens_hbm, gath.at[me, pl.ds(HEADER, length)], load_sem.at[0]
    )
    load_tokens.start()
    load_wqkv = pltpu.make_async_copy(wqkv_hbm, wqkv, load_sem.at[1])
    load_wqkv.start()
    load_wout = [
        pltpu.make_async_copy(
            wout_hbm.at[:, pl.ds(d * width, width)], wout.at[d], load_sem.at[2 + d]
        )
        for d in range(blocks)
    ]
    for load in load_wout:
        load.start()

    barrier = pltpu.get_barrier_semaphore()
    for device in (to_a, to_b, to_sib):
        pl.semaphore_signal(barrier, inc=1, device_id=device, device_id_type=MESH)
    for step in range(1, reach + 1):

        @pl.when(t + step < tok_size)
        def _():
            pl.semaphore_signal(barrier, inc=1, device_id={"tok": t + step}, device_id_type=MESH)

        @pl.when(t >= step)
        def _():
            pl.semaphore_signal(barrier, inc=1, device_id={"tok": t - step}, device_id_type=MESH)

    gath[me, 0:HEADER, :] = jnp.broadcast_to(
        gain_ref[...].astype(jnp.float32), (HEADER, width)
    ).astype(jnp.bfloat16)
    docs = docs_ref[...].astype(jnp.float32)
    pair = 2 * HEAD_SIZE
    row_index = lax.broadcasted_iota(jnp.int32, (HEADER, pair), 0)
    packed = jnp.zeros((HEADER, pair), jnp.float32)
    for i in range(length // pair):
        packed = jnp.where(row_index == i, docs[:, i * pair : (i + 1) * pair], packed)
    kvs[0, length : length + HEADER, :] = packed.astype(jnp.bfloat16)

    later = jnp.minimum(reach, tok_size - 1 - t)
    earlier = jnp.minimum(reach, t)
    pl.semaphore_wait(barrier, 3 + later + earlier)

    sent = []

    def piece(d, r):
        if r == 0:
            return gath.at[d, pl.ds(0, HEADER + rows)]
        return gath.at[d, pl.ds(HEADER + r * rows, rows)]

    kinds = (
        (me, to_a, ha * 2 + c),
        (me, to_b, hb * 2 + c),
        (ha * 2 + c, to_b, hd * 2 + c),
        (me, to_sib, h * 2 + s),
        (ha * 2 + c, to_sib, hb * 2 + s),
        (hb * 2 + c, to_sib, ha * 2 + s),
        (hd * 2 + c, to_sib, hd * 2 + s),
    )

    def ag_copy(kind, r, block):
        return pltpu.make_async_remote_copy(
            src_ref=piece(block, r),
            dst_ref=piece(block, r),
            send_sem=ag_send.at[kind, r],
            recv_sem=ag_recv.at[kind, r],
            device_id=kinds[kind][1],
            device_id_type=MESH,
        )

    def go(kind, r):
        copy = ag_copy(kind, r, kinds[kind][0])
        copy.start()
        sent.append(copy)

    def got(kind, r):
        ag_copy(kind, r, kinds[kind][2]).wait_recv()

    def own(r):
        for kind in (0, 1, 3):
            go(kind, r)

    def relay(r):
        got(0, r)
        go(2, r)
        go(4, r)
        got(1, r)
        go(5, r)

    base = base_ref[t]
    base_cos, base_sin = base[0:1, :], base[1:2, :]

    def project(r):
        where = pl.ds(HEADER + r * rows, rows)

        def square(d, held):
            x = gath[d, where, :].astype(jnp.float32)
            return held + jnp.sum(x * x, axis=1, keepdims=True)

        squares = lax.fori_loop(0, blocks, square, jnp.zeros((rows, 1), jnp.float32))
        inverse = lax.rsqrt(squares * (1.0 / (blocks * width)) + epsilon)
        mixed[...] = jnp.zeros_like(mixed)

        def multiply(d, _):
            gain = gath[d, 0:HEADER, :].astype(jnp.float32)[0:1, :]
            x = gath[d, where, :].astype(jnp.float32)
            normed = (x * inverse * gain).astype(jnp.bfloat16)
            mixed[...] += jnp.dot(normed, wqkv[d], preferred_element_type=jnp.float32)
            return 0

        lax.fori_loop(0, blocks, multiply, 0)
        span = slice(r * rows, (r + 1) * rows)
        local_cos, local_sin = local_ref[0, span, :], local_ref[1, span, :]
        cosine = local_cos * base_cos - local_sin * base_sin
        sine = local_sin * base_cos + local_cos * base_sin

        def turned(j):
            v = mixed[:, j * HEAD_SIZE : (j + 1) * HEAD_SIZE]
            return (v * cosine + pltpu.roll(v, HEAD_SIZE // 2, 1) * sine).astype(jnp.bfloat16)

        for j in range(GROUP):
            queries[r, j * rows : (j + 1) * rows, :] = turned(j)
        kvs[0, span, 0:HEAD_SIZE] = turned(GROUP)
        kvs[0, span, HEAD_SIZE:] = mixed[:, (GROUP + 1) * HEAD_SIZE :].astype(jnp.bfloat16)

    def kv_piece(slot, r):
        return kvs.at[slot, pl.ds(r * rows, rows + (HEADER if r == CHUNKS - 1 else 0))]

    def kv_copy(step, r, source):
        return pltpu.make_async_remote_copy(
            src_ref=kv_piece(source, r),
            dst_ref=kv_piece(step, r),
            send_sem=kv_send.at[step - 1, r],
            recv_sem=kv_recv.at[step - 1, r],
            device_id={"tok": (t + step) % tok_size},
            device_id_type=MESH,
        )

    power = HEAD_SIZE ** (-0.5) * float(np.log2(np.e))

    def key_docs(slot):
        held = kvs[slot, length : length + HEADER, :].astype(jnp.float32)
        return jnp.concatenate([held[i : i + 1, :] for i in range(length // pair)], axis=1)

    for r in range(CHUNKS):
        line = docs[:, r * rows : (r + 1) * rows]
        owners[r] = jnp.transpose(jnp.broadcast_to(line, (rows, rows)))[:, 0:1]

    def attend(r, slot, first):
        count = (r + 1) * rows if first else length
        q = queries[r]
        k = kvs[slot, 0:count, 0:HEAD_SIZE]
        v = kvs[slot, 0:count, HEAD_SIZE:]
        scores = lax.dot_general(
            q, k, (((1,), (1,)), ((), ())), preferred_element_type=jnp.float32
        )
        mask = key_docs(slot)[:, 0:count] == owners[r]
        if first:
            mask = mask & (
                lax.broadcasted_iota(jnp.int32, (rows, count), 1)
                <= lax.broadcasted_iota(jnp.int32, (rows, count), 0) + r * rows
            )
        scores = jnp.where(mask[None], scores.reshape(GROUP, rows, count), floor_score)
        scores = scores.reshape(GROUP * rows, count)
        high = jnp.max(scores, axis=1, keepdims=True)
        if not first:
            high = jnp.maximum(high, highs[r])
        weights = jnp.exp2((scores - high) * power)
        total = jnp.sum(weights, axis=1, keepdims=True)
        summed = jnp.dot(weights.astype(jnp.bfloat16), v, preferred_element_type=jnp.float32)
        if not first:
            fade = jnp.exp2((highs[r] - high) * power)
            total = total + totals[r] * fade
            summed = summed + accums[r] * fade
        highs[r] = high
        totals[r] = total
        accums[r] = summed

    load_tokens.wait()
    own(0)
    own(1)
    relay(0)
    load_wqkv.wait()
    for r in range(CHUNKS):
        if r + 2 < CHUNKS:
            own(r + 2)
        if r + 1 < CHUNKS:
            relay(r + 1)
        got(2, r)
        go(6, r)
        for kind in (3, 4, 5, 6):
            got(kind, r)
        project(r)

        @pl.loop(1, later + 1)
        def _(step):
            kv_copy(step, r, 0).start()

        attend(r, 0, True)

    def sib_copy(r):
        return pltpu.make_async_remote_copy(
            src_ref=sib_out.at[r], dst_ref=sib_in.at[r], send_sem=sib_send.at[r],
            recv_sem=sib_recv.at[r], device_id=to_sib, device_id_type=MESH,
        )

    def x_copy(r, i):
        return pltpu.make_async_remote_copy(
            src_ref=x_out.at[r, i], dst_ref=x_in.at[r, i], send_sem=x_send.at[r, i],
            recv_sem=x_recv.at[r, i], device_id=to_a if i == 2 else to_b, device_id_type=MESH,
        )

    def start(copy):
        copy.start()
        sent.append(copy)

    def project_out(r):
        normal = (accums[r] / totals[r]).astype(jnp.bfloat16)
        heads = jnp.concatenate([normal[j * rows : (j + 1) * rows] for j in range(GROUP)], axis=1)

        def for_sib(q, _):
            sib_out[r, q] = jnp.dot(
                heads, wout[q * 2 + s], preferred_element_type=jnp.float32
            ).astype(jnp.bfloat16)
            return 0

        lax.fori_loop(0, chips, for_sib, 0)
        start(sib_copy(r))

        def for_own(q, _):
            part[r, q] = jnp.dot(heads, wout[q * 2 + c], preferred_element_type=jnp.float32)
            return 0

        lax.fori_loop(0, chips, for_own, 0)

    def both(r, q):
        return part[r, q] + sib_in[r, q].astype(jnp.float32)

    def stage_one(r):
        sib_copy(r).wait_recv()
        for i, q in enumerate((hd, hb)):
            x_out[r, i] = both(r, q).astype(jnp.bfloat16)
            start(x_copy(r, i))

    def stage_two(r):
        x_copy(r, 0).wait_recv()
        x_out[r, 2] = (both(r, ha) + x_in[r, 0].astype(jnp.float32)).astype(jnp.bfloat16)
        start(x_copy(r, 2))

    def stage_three(r):
        x_copy(r, 1).wait_recv()
        x_copy(r, 2).wait_recv()
        out_ref[r * rows : (r + 1) * rows, :] = (
            both(r, h) + x_in[r, 1].astype(jnp.float32) + x_in[r, 2].astype(jnp.float32)
        ).astype(jnp.bfloat16)

    @pl.loop(1, jnp.minimum(reach - 1, t) + 1)
    def _(step):
        for r in range(CHUNKS):
            kv_copy(step, r, step).wait_recv()

        @pl.loop(0, CHUNKS)
        def _(r):
            attend(r, step, False)

    @pl.when(t >= reach)
    def _():
        for r in range(CHUNKS):
            kv_copy(reach, r, reach).wait_recv()

    for load in load_wout:
        load.wait()
    for r in range(CHUNKS + 3):
        if r < CHUNKS:

            @pl.when(t >= reach)
            def _():
                attend(r, reach, False)

            project_out(r)
        if 0 <= r - 1 < CHUNKS:
            stage_one(r - 1)
        if 0 <= r - 2 < CHUNKS:
            stage_two(r - 2)
        if 0 <= r - 3 < CHUNKS:
            stage_three(r - 3)

    for copy in sent:
        copy.wait_send()
    @pl.loop(1, later + 1)
    def _(step):
        for r in range(CHUNKS):
            kv_copy(step, r, 0).wait_send()


def tables(length, tok_size):
    half = HEAD_SIZE // 2
    inverse = theta ** (-np.arange(half, dtype=np.float64) * (2.0 / HEAD_SIZE))

    def pair(positions):
        angles = positions[:, None] * inverse[None, :]
        cosine, sine = np.cos(angles), np.sin(angles)
        return np.stack(
            [np.concatenate([cosine, cosine], 1), np.concatenate([-sine, sine], 1)]
        ).astype(np.float32)

    local = pair(np.arange(length, dtype=np.float64))
    base = pair(np.arange(tok_size, dtype=np.float64) * length).transpose(1, 0, 2)
    return jnp.asarray(local), jnp.asarray(base)


def body(mesh_shape, tokens, norm_gain, query_key_value_weight, out_weight, doc_ids):
    tok_size = mesh_shape["tok"]
    blocks = mesh_shape["head"] * mesh_shape["grp"]
    chips = blocks // 2
    reach = tok_size // 2
    length, width = tokens.shape
    rows = length // CHUNKS
    columns = query_key_value_weight.shape[1]
    local, base = tables(length, tok_size)
    bf16, f32 = jnp.bfloat16, jnp.float32
    vmem = pl.BlockSpec(memory_space=pltpu.VMEM)
    hbm = pl.BlockSpec(memory_space=pl.ANY)
    dma = pltpu.SemaphoreType.DMA
    return pl.pallas_call(
        functools.partial(kernel, tok_size),
        out_shape=jax.ShapeDtypeStruct((length, width), bf16),
        in_specs=[hbm, vmem, hbm, hbm, vmem, vmem, vmem],
        out_specs=vmem,
        scratch_shapes=[
            pltpu.VMEM((blocks, HEADER + length, width), bf16),
            pltpu.VMEM((blocks, width, columns), bf16),
            pltpu.VMEM((blocks, out_weight.shape[0], width), bf16),
            pltpu.VMEM((CHUNKS, GROUP * rows, HEAD_SIZE), bf16),
            pltpu.VMEM((1 + reach, length + HEADER, 2 * HEAD_SIZE), bf16),
            pltpu.VMEM((rows, columns), f32),
            pltpu.VMEM((CHUNKS, rows, 1), f32),
            pltpu.VMEM((CHUNKS, GROUP * rows, 1), f32),
            pltpu.VMEM((CHUNKS, GROUP * rows, 1), f32),
            pltpu.VMEM((CHUNKS, GROUP * rows, HEAD_SIZE), f32),
            pltpu.VMEM((CHUNKS, chips, rows, width), bf16),
            pltpu.VMEM((CHUNKS, chips, rows, width), bf16),
            pltpu.VMEM((CHUNKS, chips, rows, width), f32),
            pltpu.VMEM((CHUNKS, 3, rows, width), bf16),
            pltpu.VMEM((CHUNKS, 3, rows, width), bf16),
            dma((2 + blocks,)),
            dma((7, CHUNKS)),
            dma((7, CHUNKS)),
            dma((reach, CHUNKS)),
            dma((reach, CHUNKS)),
            dma((CHUNKS,)),
            dma((CHUNKS,)),
            dma((CHUNKS, 3)),
            dma((CHUNKS, 3)),
        ],
        compiler_params=pltpu.CompilerParams(
            collective_id=0, has_side_effects=True, vmem_limit_bytes=58 * 2**20
        ),
    )(
        tokens,
        norm_gain.reshape(1, width),
        query_key_value_weight.reshape(blocks, width, columns),
        out_weight,
        doc_ids.reshape(1, length),
        local,
        base,
    )


def solution(mesh):
    return jax.shard_map(
        functools.partial(body, dict(mesh.shape)),
        mesh=mesh,
        in_specs=(
            P("tok", ("head", "grp")),
            P(("head", "grp")),
            P(None, ("head", "grp")),
            P(("head", "grp"), None),
            P("tok"),
        ),
        out_specs=P("tok", ("head", "grp")),
        check_vma=False,
    )
```

```python
import functools

import jax
import jax.numpy as jnp
import numpy as np
from jax import lax
from jax.experimental import pallas as pl
from jax.experimental.pallas import tpu as pltpu
from jax.sharding import PartitionSpec as P

QUERY_HEADS = 32
KEY_VALUE_HEADS = 8
HEAD_SIZE = 128
GROUP = QUERY_HEADS // KEY_VALUE_HEADS

epsilon = 1e-05
theta = 500000.0
floor_score = -1e30
HEADER = 16
CHUNKS = 4
MESH = pl.DeviceIdType.MESH


def kernel(
    size, tokens_hbm, gain_ref, wqkv_hbm, wout_hbm, docs_ref, local_ref, base_ref, out_ref,
    gath, wqkv, wout, queries, kvs, mixed, owners, highs, totals, accums,
    sib_out, sib_in, part, x_out, x_in,
    load_sem, ag_send, ag_recv, kv_send, kv_recv, sib_send, sib_recv, x_send, x_recv,
):
    tok_size, reach = size, size // 2
    length, width = tokens_hbm.shape
    blocks = gath.shape[0]
    chips = blocks // 2
    rows = length // CHUNKS
    t = lax.axis_index("tok")
    h = lax.axis_index("head")
    c = lax.axis_index("grp")
    hx = h + 1 - 2 * (h % 2)
    hy = h + 2 - 4 * ((h // 2) % 2)
    ha = hx * (1 - c) + hy * c
    hb = hy * (1 - c) + hx * c
    hd = hx + hy - h
    s = 1 - c
    me = h * 2 + c
    to_a, to_b, to_sib = {"head": ha}, {"head": hb}, {"grp": s}

    load_tokens = pltpu.make_async_copy(
        tokens_hbm, gath.at[me, pl.ds(HEADER, length)], load_sem.at[0]
    )
    load_tokens.start()
    load_wqkv = pltpu.make_async_copy(wqkv_hbm, wqkv, load_sem.at[1])
    load_wqkv.start()
    load_wout = [
        pltpu.make_async_copy(
            wout_hbm.at[:, pl.ds(d * width, width)], wout.at[d], load_sem.at[2 + d]
        )
        for d in range(blocks)
    ]
    for load in load_wout:
        load.start()

    barrier = pltpu.get_barrier_semaphore()
    for device in (to_a, to_b, to_sib):
        pl.semaphore_signal(barrier, inc=1, device_id=device, device_id_type=MESH)
    @pl.when(t + 1 < tok_size)
    def _():
        pl.semaphore_signal(barrier, inc=1, device_id={"tok": t + 1}, device_id_type=MESH)

    @pl.when(t >= 1)
    def _():
        pl.semaphore_signal(barrier, inc=1, device_id={"tok": t - 1}, device_id_type=MESH)

    gath[me, 0:HEADER, :] = jnp.broadcast_to(
        gain_ref[...].astype(jnp.float32).reshape(1, width), (HEADER, width)
    ).astype(jnp.bfloat16)
    docs = docs_ref[...].astype(jnp.float32)
    pair = 2 * HEAD_SIZE
    row_index = lax.broadcasted_iota(jnp.int32, (HEADER, pair), 0)
    packed = jnp.zeros((HEADER, pair), jnp.float32)
    for i in range(length // pair):
        packed = jnp.where(row_index == i, docs[:, i * pair : (i + 1) * pair], packed)
    kvs[0, length : length + HEADER, :] = packed.astype(jnp.bfloat16)

    later = jnp.minimum(1, tok_size - 1 - t)
    earlier = jnp.minimum(1, t)
    pl.semaphore_wait(barrier, 3 + later + earlier)

    sent = []

    def piece(d, r):
        if r == 0:
            return gath.at[d, pl.ds(0, HEADER + rows)]
        return gath.at[d, pl.ds(HEADER + r * rows, rows)]

    kinds = (
        (me, to_a, ha * 2 + c),
        (me, to_b, hb * 2 + c),
        (ha * 2 + c, to_b, hd * 2 + c),
        (me, to_sib, h * 2 + s),
        (ha * 2 + c, to_sib, hb * 2 + s),
        (hb * 2 + c, to_sib, ha * 2 + s),
        (hd * 2 + c, to_sib, hd * 2 + s),
    )

    def ag_copy(kind, r, block):
        return pltpu.make_async_remote_copy(
            src_ref=piece(block, r),
            dst_ref=piece(block, r),
            send_sem=ag_send.at[kind, r],
            recv_sem=ag_recv.at[kind, r],
            device_id=kinds[kind][1],
            device_id_type=MESH,
        )

    def go(kind, r):
        copy = ag_copy(kind, r, kinds[kind][0])
        copy.start()
        sent.append(copy)

    def got(kind, r):
        ag_copy(kind, r, kinds[kind][2]).wait_recv()

    def own(r):
        for kind in (0, 1, 3):
            go(kind, r)

    def relay(r):
        got(0, r)
        go(2, r)
        go(4, r)
        got(1, r)
        go(5, r)

    base = base_ref[t]
    base_cos, base_sin = base[0:1, :], base[1:2, :]

    def project(r):
        where = pl.ds(HEADER + r * rows, rows)

        def square(d, held):
            x = gath[d, where, :].astype(jnp.float32)
            return held + jnp.sum(x * x, axis=1, keepdims=True)

        squares = lax.fori_loop(0, blocks, square, jnp.zeros((rows, 1), jnp.float32), unroll=True)
        inverse = lax.rsqrt(squares * (1.0 / (blocks * width)) + epsilon)
        mixed[...] = jnp.zeros_like(mixed)

        def multiply(d, _):
            gain = gath[d, 0:HEADER, :].astype(jnp.float32)[0:1, :]
            x = gath[d, where, :].astype(jnp.float32)
            normed = (x * inverse * gain).astype(jnp.bfloat16)
            mixed[...] += jnp.dot(normed, wqkv[d], preferred_element_type=jnp.float32)
            return 0

        lax.fori_loop(0, blocks, multiply, 0, unroll=True)
        span = slice(r * rows, (r + 1) * rows)
        local_cos, local_sin = local_ref[0, span, :], local_ref[1, span, :]
        cosine = local_cos * base_cos - local_sin * base_sin
        sine = local_sin * base_cos + local_cos * base_sin

        def turned(j):
            v = mixed[:, j * HEAD_SIZE : (j + 1) * HEAD_SIZE]
            return (v * cosine + pltpu.roll(v, HEAD_SIZE // 2, 1) * sine).astype(jnp.bfloat16)

        for j in range(GROUP):
            queries[r, j * rows : (j + 1) * rows, :] = turned(j)
        kvs[0, span, 0:HEAD_SIZE] = turned(GROUP)
        kvs[0, span, HEAD_SIZE:] = mixed[:, (GROUP + 1) * HEAD_SIZE :].astype(jnp.bfloat16)

    def kv_piece(slot, r):
        return kvs.at[slot, pl.ds(r * rows, rows + (HEADER if r == CHUNKS - 1 else 0))]

    def kv_copy(step, r):
        return pltpu.make_async_remote_copy(
            src_ref=kv_piece(step - 1, r),
            dst_ref=kv_piece(step, r),
            send_sem=kv_send.at[step - 1, r],
            recv_sem=kv_recv.at[step - 1, r],
            device_id={"tok": (t + 1) % tok_size},
            device_id_type=MESH,
        )

    def relay_kv(step, r):
        @pl.when(t >= step)
        def _():
            kv_copy(step, r).wait_recv()

        if not isinstance(step, int) or step < reach:

            @pl.when((t >= step) & (t + 1 < tok_size))
            def _():
                kv_copy(step + 1, r).start()

    power = HEAD_SIZE ** (-0.5) * float(np.log2(np.e))

    def key_docs(slot):
        held = kvs[slot, length : length + HEADER, :].astype(jnp.float32)
        return jnp.concatenate([held[i : i + 1, :] for i in range(length // pair)], axis=1)

    for i in range(length // HEAD_SIZE):
        line = docs[:, i * HEAD_SIZE : (i + 1) * HEAD_SIZE]
        square_of = jnp.transpose(jnp.broadcast_to(line, (HEAD_SIZE, HEAD_SIZE)))
        owners[i * HEAD_SIZE : (i + 1) * HEAD_SIZE, :] = square_of[:, 0:1]

    def attend(r, slot, first):
        count = (r + 1) * rows if first else length
        q = queries[r]
        k = kvs[slot, 0:count, 0:HEAD_SIZE]
        v = kvs[slot, 0:count, HEAD_SIZE:]
        scores = lax.dot_general(
            q, k, (((1,), (1,)), ((), ())), preferred_element_type=jnp.float32
        )
        mask = key_docs(slot)[:, 0:count] == owners[pl.ds(r * rows, rows), :]
        if first:
            mask = mask & (
                lax.broadcasted_iota(jnp.int32, (rows, count), 1)
                <= lax.broadcasted_iota(jnp.int32, (rows, count), 0) + r * rows
            )
        scores = jnp.where(mask[None], scores.reshape(GROUP, rows, count), floor_score)
        scores = scores.reshape(GROUP * rows, count)
        high = jnp.max(scores, axis=1, keepdims=True)
        if not first:
            high = jnp.maximum(high, highs[r])
        weights = jnp.exp2((scores - high) * power)
        total = jnp.sum(weights, axis=1, keepdims=True)
        summed = jnp.dot(weights.astype(jnp.bfloat16), v, preferred_element_type=jnp.float32)
        if not first:
            fade = jnp.exp2((highs[r] - high) * power)
            total = total + totals[r] * fade
            summed = summed + accums[r] * fade
        highs[r] = high
        totals[r] = total
        accums[r] = summed

    load_tokens.wait()
    own(0)
    own(1)
    relay(0)
    load_wqkv.wait()
    for r in range(CHUNKS):
        if r + 2 < CHUNKS:
            own(r + 2)
        if r + 1 < CHUNKS:
            relay(r + 1)
        got(2, r)
        go(6, r)
        for kind in (3, 4, 5, 6):
            got(kind, r)
        project(r)

        @pl.when(t + 1 < tok_size)
        def _():
            kv_copy(1, r).start()

        if r >= 1:
            relay_kv(1, r - 1)

        attend(r, 0, True)

    def sib_copy(r):
        return pltpu.make_async_remote_copy(
            src_ref=sib_out.at[r], dst_ref=sib_in.at[r], send_sem=sib_send.at[r],
            recv_sem=sib_recv.at[r], device_id=to_sib, device_id_type=MESH,
        )

    def x_copy(r, i):
        return pltpu.make_async_remote_copy(
            src_ref=x_out.at[r, i], dst_ref=x_in.at[r, i], send_sem=x_send.at[r, i],
            recv_sem=x_recv.at[r, i], device_id=to_a if i == 2 else to_b, device_id_type=MESH,
        )

    def start(copy):
        copy.start()
        sent.append(copy)

    def project_out(r):
        normal = (accums[r] / totals[r]).astype(jnp.bfloat16)
        heads = jnp.concatenate([normal[j * rows : (j + 1) * rows] for j in range(GROUP)], axis=1)

        def for_sib(q, _):
            sib_out[r, q] = jnp.dot(
                heads, wout[q * 2 + s], preferred_element_type=jnp.float32
            ).astype(jnp.bfloat16)
            return 0

        lax.fori_loop(0, chips, for_sib, 0)
        start(sib_copy(r))

        def for_own(q, _):
            part[r, q] = jnp.dot(heads, wout[q * 2 + c], preferred_element_type=jnp.float32)
            return 0

        lax.fori_loop(0, chips, for_own, 0)

    def both(r, q):
        return part[r, q] + sib_in[r, q].astype(jnp.float32)

    def stage_one(r):
        sib_copy(r).wait_recv()
        for i, q in enumerate((hd, hb)):
            x_out[r, i] = both(r, q).astype(jnp.bfloat16)
            start(x_copy(r, i))

    def stage_two(r):
        x_copy(r, 0).wait_recv()
        x_out[r, 2] = (both(r, ha) + x_in[r, 0].astype(jnp.float32)).astype(jnp.bfloat16)
        start(x_copy(r, 2))

    def stage_three(r):
        x_copy(r, 1).wait_recv()
        x_copy(r, 2).wait_recv()
        out_ref[r * rows : (r + 1) * rows, :] = (
            both(r, h) + x_in[r, 1].astype(jnp.float32) + x_in[r, 2].astype(jnp.float32)
        ).astype(jnp.bfloat16)

    relay_kv(1, CHUNKS - 1)

    @pl.loop(1, reach)
    def _(step):
        @pl.when(step >= 2)
        def _():
            for r in range(CHUNKS):
                relay_kv(step, r)

        @pl.when(t >= step)
        def _():
            @pl.loop(0, CHUNKS)
            def _(r):
                attend(r, step, False)

    if reach >= 2:
        for r in range(CHUNKS):
            relay_kv(reach, r)

    for load in load_wout:
        load.wait()
    for r in range(CHUNKS + 3):
        if r < CHUNKS:

            @pl.when(t >= reach)
            def _():
                attend(r, reach, False)

            project_out(r)
        if 0 <= r - 1 < CHUNKS:
            stage_one(r - 1)
        if 0 <= r - 2 < CHUNKS:
            stage_two(r - 2)
        if 0 <= r - 3 < CHUNKS:
            stage_three(r - 3)

    for copy in sent:
        copy.wait_send()
    @pl.loop(1, reach + 1)
    def _(step):
        @pl.when((t >= step - 1) & (t + 1 < tok_size))
        def _():
            for r in range(CHUNKS):
                kv_copy(step, r).wait_send()


def tables(length, tok_size):
    half = HEAD_SIZE // 2
    inverse = theta ** (-np.arange(half, dtype=np.float64) * (2.0 / HEAD_SIZE))

    def pair(positions):
        angles = positions[:, None] * inverse[None, :]
        cosine, sine = np.cos(angles), np.sin(angles)
        return np.stack(
            [np.concatenate([cosine, cosine], 1), np.concatenate([-sine, sine], 1)]
        ).astype(np.float32)

    local = pair(np.arange(length, dtype=np.float64))
    base = pair(np.arange(tok_size, dtype=np.float64) * length).transpose(1, 0, 2)
    return jnp.asarray(local), jnp.asarray(base)


def body(mesh_shape, tokens, norm_gain, query_key_value_weight, out_weight, doc_ids):
    tok_size = mesh_shape["tok"]
    blocks = mesh_shape["head"] * mesh_shape["grp"]
    chips = blocks // 2
    reach = tok_size // 2
    length, width = tokens.shape
    rows = length // CHUNKS
    columns = query_key_value_weight.shape[1]
    local, base = tables(length, tok_size)
    bf16, f32 = jnp.bfloat16, jnp.float32
    vmem = pl.BlockSpec(memory_space=pltpu.VMEM)
    hbm = pl.BlockSpec(memory_space=pl.ANY)
    dma = pltpu.SemaphoreType.DMA
    return pl.pallas_call(
        functools.partial(kernel, tok_size),
        out_shape=jax.ShapeDtypeStruct((length, width), bf16),
        in_specs=[hbm, vmem, hbm, hbm, vmem, vmem, vmem],
        out_specs=vmem,
        scratch_shapes=[
            pltpu.VMEM((blocks, HEADER + length, width), bf16),
            pltpu.VMEM((blocks, width, columns), bf16),
            pltpu.VMEM((blocks, out_weight.shape[0], width), bf16),
            pltpu.VMEM((CHUNKS, GROUP * rows, HEAD_SIZE), bf16),
            pltpu.VMEM((1 + reach, length + HEADER, 2 * HEAD_SIZE), bf16),
            pltpu.VMEM((rows, columns), f32),
            pltpu.VMEM((length, 1), f32),
            pltpu.VMEM((CHUNKS, GROUP * rows, 1), f32),
            pltpu.VMEM((CHUNKS, GROUP * rows, 1), f32),
            pltpu.VMEM((CHUNKS, GROUP * rows, HEAD_SIZE), f32),
            pltpu.VMEM((CHUNKS, chips, rows, width), bf16),
            pltpu.VMEM((CHUNKS, chips, rows, width), bf16),
            pltpu.VMEM((CHUNKS, chips, rows, width), f32),
            pltpu.VMEM((CHUNKS, 3, rows, width), bf16),
            pltpu.VMEM((CHUNKS, 3, rows, width), bf16),
            dma((2 + blocks,)),
            dma((7, CHUNKS)),
            dma((7, CHUNKS)),
            dma((reach, CHUNKS)),
            dma((reach, CHUNKS)),
            dma((CHUNKS,)),
            dma((CHUNKS,)),
            dma((CHUNKS, 3)),
            dma((CHUNKS, 3)),
        ],
        compiler_params=pltpu.CompilerParams(
            collective_id=0, has_side_effects=True, vmem_limit_bytes=58 * 2**20
        ),
    )(
        tokens,
        norm_gain,
        query_key_value_weight.reshape(blocks, width, columns),
        out_weight,
        doc_ids.reshape(1, length),
        local,
        base,
    )


def solution(mesh):
    return jax.shard_map(
        functools.partial(body, dict(mesh.shape)),
        mesh=mesh,
        in_specs=(
            P("tok", ("head", "grp")),
            P(("head", "grp")),
            P(None, ("head", "grp")),
            P(("head", "grp"), None),
            P("tok"),
        ),
        out_specs=P("tok", ("head", "grp")),
        check_vma=False,
    )
```

```python
import functools

import jax
import jax.numpy as jnp
import numpy as np
from jax import lax
from jax.experimental import pallas as pl
from jax.experimental.pallas import tpu as pltpu
from jax.sharding import PartitionSpec as P

QUERY_HEADS = 32
KEY_VALUE_HEADS = 8
HEAD_SIZE = 128
GROUP = QUERY_HEADS // KEY_VALUE_HEADS

epsilon = 1e-05
theta = 500000.0
floor_score = -1e30
HEADER = 16
CHUNKS = 4
MESH = pl.DeviceIdType.MESH


def kernel(
    size, tokens_hbm, gain_ref, wqkv_hbm, wout_hbm, docs_ref, local_ref, base_ref, out_ref,
    gath, wqkv, wout, queries, kvs, mixed, owners, highs, totals, accums,
    sib_out, sib_in, part, x_out, x_in,
    load_sem, ag_send, ag_recv, kv_send, kv_recv, sib_send, sib_recv, x_send, x_recv,
):
    tok_size, reach = size, size // 2
    length, width = tokens_hbm.shape
    blocks = gath.shape[0]
    chips = blocks // 2
    rows = length // CHUNKS
    t = lax.axis_index("tok")
    h = lax.axis_index("head")
    c = lax.axis_index("grp")
    hx = h + 1 - 2 * (h % 2)
    hy = h + 2 - 4 * ((h // 2) % 2)
    ha = hx * (1 - c) + hy * c
    hb = hy * (1 - c) + hx * c
    hd = hx + hy - h
    s = 1 - c
    me = h * 2 + c
    to_a, to_b, to_sib = {"head": ha}, {"head": hb}, {"grp": s}

    load_tokens = pltpu.make_async_copy(
        tokens_hbm, gath.at[me, pl.ds(HEADER, length)], load_sem.at[0]
    )
    load_tokens.start()
    load_wqkv = pltpu.make_async_copy(wqkv_hbm, wqkv, load_sem.at[1])
    load_wqkv.start()
    load_wout = [
        pltpu.make_async_copy(
            wout_hbm.at[:, pl.ds(d * width, width)], wout.at[d], load_sem.at[2 + d]
        )
        for d in range(blocks)
    ]
    for load in load_wout:
        load.start()

    barrier = pltpu.get_barrier_semaphore()
    for device in (to_a, to_b, to_sib):
        pl.semaphore_signal(barrier, inc=1, device_id=device, device_id_type=MESH)
    @pl.when(t + 1 < tok_size)
    def _():
        pl.semaphore_signal(barrier, inc=1, device_id={"tok": t + 1}, device_id_type=MESH)

    @pl.when(t >= 1)
    def _():
        pl.semaphore_signal(barrier, inc=1, device_id={"tok": t - 1}, device_id_type=MESH)

    gath[me, 0:HEADER, :] = jnp.broadcast_to(
        gain_ref[...].astype(jnp.float32).reshape(1, width), (HEADER, width)
    ).astype(jnp.bfloat16)
    docs = docs_ref[...].astype(jnp.float32)
    pair = 2 * HEAD_SIZE
    row_index = lax.broadcasted_iota(jnp.int32, (HEADER, pair), 0)
    packed = jnp.zeros((HEADER, pair), jnp.float32)
    for i in range(length // pair):
        packed = jnp.where(row_index == i, docs[:, i * pair : (i + 1) * pair], packed)
    kvs[0, length : length + HEADER, :] = packed.astype(jnp.bfloat16)

    later = jnp.minimum(1, tok_size - 1 - t)
    earlier = jnp.minimum(1, t)
    pl.semaphore_wait(barrier, 3 + later + earlier)

    sent = []

    def piece(d, r):
        if r == 0:
            return gath.at[d, pl.ds(0, HEADER + rows)]
        return gath.at[d, pl.ds(HEADER + r * rows, rows)]

    kinds = (
        (me, to_a, ha * 2 + c),
        (me, to_b, hb * 2 + c),
        (ha * 2 + c, to_b, hd * 2 + c),
        (me, to_sib, h * 2 + s),
        (ha * 2 + c, to_sib, hb * 2 + s),
        (hb * 2 + c, to_sib, ha * 2 + s),
        (hd * 2 + c, to_sib, hd * 2 + s),
    )

    def ag_copy(kind, r, block):
        return pltpu.make_async_remote_copy(
            src_ref=piece(block, r),
            dst_ref=piece(block, r),
            send_sem=ag_send.at[kind, r],
            recv_sem=ag_recv.at[kind, r],
            device_id=kinds[kind][1],
            device_id_type=MESH,
        )

    def go(kind, r):
        copy = ag_copy(kind, r, kinds[kind][0])
        copy.start()
        sent.append(copy)

    def got(kind, r):
        ag_copy(kind, r, kinds[kind][2]).wait_recv()

    def own(r):
        for kind in (0, 1, 3):
            go(kind, r)

    def relay(r):
        got(0, r)
        go(2, r)
        go(4, r)
        got(1, r)
        go(5, r)

    base = base_ref[t]
    base_cos, base_sin = base[0:1, :], base[1:2, :]

    def project(r):
        where = pl.ds(HEADER + r * rows, rows)

        def square(d, held):
            x = gath[d, where, :].astype(jnp.float32)
            return held + jnp.sum(x * x, axis=1, keepdims=True)

        squares = lax.fori_loop(0, blocks, square, jnp.zeros((rows, 1), jnp.float32), unroll=True)
        inverse = lax.rsqrt(squares * (1.0 / (blocks * width)) + epsilon)
        mixed[...] = jnp.zeros_like(mixed)

        def multiply(d, _):
            gain = gath[d, 0:HEADER, :].astype(jnp.float32)[0:1, :]
            x = gath[d, where, :].astype(jnp.float32)
            normed = (x * inverse * gain).astype(jnp.bfloat16)
            mixed[...] += jnp.dot(normed, wqkv[d], preferred_element_type=jnp.float32)
            return 0

        lax.fori_loop(0, blocks, multiply, 0, unroll=True)
        span = slice(r * rows, (r + 1) * rows)
        local_cos, local_sin = local_ref[0, span, :], local_ref[1, span, :]
        cosine = local_cos * base_cos - local_sin * base_sin
        sine = local_sin * base_cos + local_cos * base_sin

        def turned(j):
            v = mixed[:, j * HEAD_SIZE : (j + 1) * HEAD_SIZE]
            return (v * cosine + pltpu.roll(v, HEAD_SIZE // 2, 1) * sine).astype(jnp.bfloat16)

        for j in range(GROUP):
            queries[r, j * rows : (j + 1) * rows, :] = turned(j)
        kvs[0, span, 0:HEAD_SIZE] = turned(GROUP)
        kvs[0, span, HEAD_SIZE:] = mixed[:, (GROUP + 1) * HEAD_SIZE :].astype(jnp.bfloat16)

    def kv_piece(slot, r):
        return kvs.at[slot, pl.ds(r * rows, rows + (HEADER if r == CHUNKS - 1 else 0))]

    def kv_copy(step, r):
        return pltpu.make_async_remote_copy(
            src_ref=kv_piece(step - 1, r),
            dst_ref=kv_piece(step, r),
            send_sem=kv_send.at[step - 1, r],
            recv_sem=kv_recv.at[step - 1, r],
            device_id={"tok": (t + 1) % tok_size},
            device_id_type=MESH,
        )

    def relay_kv(step, r):
        @pl.when(t >= step)
        def _():
            kv_copy(step, r).wait_recv()

        if not isinstance(step, int) or step < reach:

            @pl.when((t >= step) & (t + 1 < tok_size))
            def _():
                kv_copy(step + 1, r).start()

    power = HEAD_SIZE ** (-0.5) * float(np.log2(np.e))

    def key_docs(slot):
        held = kvs[slot, length : length + HEADER, :].astype(jnp.float32)
        return jnp.concatenate([held[i : i + 1, :] for i in range(length // pair)], axis=1)

    for i in range(length // HEAD_SIZE):
        line = docs[:, i * HEAD_SIZE : (i + 1) * HEAD_SIZE]
        square_of = jnp.transpose(jnp.broadcast_to(line, (HEAD_SIZE, HEAD_SIZE)))
        owners[i * HEAD_SIZE : (i + 1) * HEAD_SIZE, :] = square_of[:, 0:1]

    def attend(r, slot, first):
        count = (r + 1) * rows if first else length
        q = queries[r]
        k = kvs[slot, 0:count, 0:HEAD_SIZE]
        v = kvs[slot, 0:count, HEAD_SIZE:]
        scores = lax.dot_general(
            q, k, (((1,), (1,)), ((), ())), preferred_element_type=jnp.float32
        )
        mask = key_docs(slot)[:, 0:count] == owners[pl.ds(r * rows, rows), :]
        if first:
            mask = mask & (
                lax.broadcasted_iota(jnp.int32, (rows, count), 1)
                <= lax.broadcasted_iota(jnp.int32, (rows, count), 0) + r * rows
            )
        scores = jnp.where(mask[None], scores.reshape(GROUP, rows, count), floor_score)
        scores = scores.reshape(GROUP * rows, count)
        high = jnp.max(scores, axis=1, keepdims=True)
        if not first:
            high = jnp.maximum(high, highs[r])
        weights = jnp.exp2((scores - high) * power)
        total = jnp.sum(weights, axis=1, keepdims=True)
        summed = jnp.dot(weights.astype(jnp.bfloat16), v, preferred_element_type=jnp.float32)
        if not first:
            fade = jnp.exp2((highs[r] - high) * power)
            total = total + totals[r] * fade
            summed = summed + accums[r] * fade
        highs[r] = high
        totals[r] = total
        accums[r] = summed

    load_tokens.wait()
    own(0)
    own(1)
    relay(0)
    load_wqkv.wait()
    for r in range(CHUNKS):
        if r + 2 < CHUNKS:
            own(r + 2)
        if r + 1 < CHUNKS:
            relay(r + 1)
        got(2, r)
        go(6, r)
        for kind in (3, 4, 5, 6):
            got(kind, r)
        project(r)

        @pl.when(t + 1 < tok_size)
        def _():
            kv_copy(1, r).start()

        if r >= 1:
            relay_kv(1, r - 1)

        attend(r, 0, True)

    def sib_copy(r):
        return pltpu.make_async_remote_copy(
            src_ref=sib_out.at[r], dst_ref=sib_in.at[r], send_sem=sib_send.at[r],
            recv_sem=sib_recv.at[r], device_id=to_sib, device_id_type=MESH,
        )

    def x_copy(r, i):
        return pltpu.make_async_remote_copy(
            src_ref=x_out.at[r, i], dst_ref=x_in.at[r, i], send_sem=x_send.at[r, i],
            recv_sem=x_recv.at[r, i], device_id=to_a if i == 2 else to_b, device_id_type=MESH,
        )

    def start(copy):
        copy.start()
        sent.append(copy)

    def project_out(r):
        normal = (accums[r] / totals[r]).astype(jnp.bfloat16)
        heads = jnp.concatenate([normal[j * rows : (j + 1) * rows] for j in range(GROUP)], axis=1)

        def for_sib(q, _):
            sib_out[r, q] = jnp.dot(
                heads, wout[q * 2 + s], preferred_element_type=jnp.float32
            ).astype(jnp.bfloat16)
            return 0

        lax.fori_loop(0, chips, for_sib, 0, unroll=True)
        start(sib_copy(r))

        def for_own(q, _):
            part[r, q] = jnp.dot(heads, wout[q * 2 + c], preferred_element_type=jnp.float32)
            return 0

        lax.fori_loop(0, chips, for_own, 0, unroll=True)

    def both(r, q):
        return part[r, q] + sib_in[r, q].astype(jnp.float32)

    def stage_one(r):
        sib_copy(r).wait_recv()
        for i, q in enumerate((hd, hb)):
            x_out[r, i] = both(r, q).astype(jnp.bfloat16)
            start(x_copy(r, i))

    def stage_two(r):
        x_copy(r, 0).wait_recv()
        x_out[r, 2] = (both(r, ha) + x_in[r, 0].astype(jnp.float32)).astype(jnp.bfloat16)
        start(x_copy(r, 2))

    def stage_three(r):
        x_copy(r, 1).wait_recv()
        x_copy(r, 2).wait_recv()
        out_ref[r * rows : (r + 1) * rows, :] = (
            both(r, h) + x_in[r, 1].astype(jnp.float32) + x_in[r, 2].astype(jnp.float32)
        ).astype(jnp.bfloat16)

    relay_kv(1, CHUNKS - 1)

    @pl.loop(1, reach)
    def _(step):
        @pl.when(step >= 2)
        def _():
            for r in range(CHUNKS):
                relay_kv(step, r)

        @pl.when(t >= step)
        def _():
            @pl.loop(0, CHUNKS)
            def _(r):
                attend(r, step, False)

    if reach >= 2:
        for r in range(CHUNKS):
            relay_kv(reach, r)

    for load in load_wout:
        load.wait()
    for r in range(CHUNKS + 3):
        if r < CHUNKS:

            @pl.when(t >= reach)
            def _():
                attend(r, reach, False)

        if 0 <= r - 1 < CHUNKS:
            stage_one(r - 1)
        if 0 <= r - 2 < CHUNKS:
            stage_two(r - 2)
        if r < CHUNKS:
            project_out(r)
        if 0 <= r - 3 < CHUNKS:
            stage_three(r - 3)

    for copy in sent:
        copy.wait_send()
    @pl.loop(1, reach + 1)
    def _(step):
        @pl.when((t >= step - 1) & (t + 1 < tok_size))
        def _():
            for r in range(CHUNKS):
                kv_copy(step, r).wait_send()


def tables(length, tok_size):
    half = HEAD_SIZE // 2
    inverse = theta ** (-np.arange(half, dtype=np.float64) * (2.0 / HEAD_SIZE))

    def pair(positions):
        angles = positions[:, None] * inverse[None, :]
        cosine, sine = np.cos(angles), np.sin(angles)
        return np.stack(
            [np.concatenate([cosine, cosine], 1), np.concatenate([-sine, sine], 1)]
        ).astype(np.float32)

    local = pair(np.arange(length, dtype=np.float64))
    base = pair(np.arange(tok_size, dtype=np.float64) * length).transpose(1, 0, 2)
    return jnp.asarray(local), jnp.asarray(base)


def body(mesh_shape, tokens, norm_gain, query_key_value_weight, out_weight, doc_ids):
    tok_size = mesh_shape["tok"]
    blocks = mesh_shape["head"] * mesh_shape["grp"]
    chips = blocks // 2
    reach = tok_size // 2
    length, width = tokens.shape
    rows = length // CHUNKS
    columns = query_key_value_weight.shape[1]
    local, base = tables(length, tok_size)
    bf16, f32 = jnp.bfloat16, jnp.float32
    vmem = pl.BlockSpec(memory_space=pltpu.VMEM)
    hbm = pl.BlockSpec(memory_space=pl.ANY)
    dma = pltpu.SemaphoreType.DMA
    return pl.pallas_call(
        functools.partial(kernel, tok_size),
        out_shape=jax.ShapeDtypeStruct((length, width), bf16),
        in_specs=[hbm, vmem, hbm, hbm, vmem, vmem, vmem],
        out_specs=vmem,
        scratch_shapes=[
            pltpu.VMEM((blocks, HEADER + length, width), bf16),
            pltpu.VMEM((blocks, width, columns), bf16),
            pltpu.VMEM((blocks, out_weight.shape[0], width), bf16),
            pltpu.VMEM((CHUNKS, GROUP * rows, HEAD_SIZE), bf16),
            pltpu.VMEM((1 + reach, length + HEADER, 2 * HEAD_SIZE), bf16),
            pltpu.VMEM((rows, columns), f32),
            pltpu.VMEM((length, 1), f32),
            pltpu.VMEM((CHUNKS, GROUP * rows, 1), f32),
            pltpu.VMEM((CHUNKS, GROUP * rows, 1), f32),
            pltpu.VMEM((CHUNKS, GROUP * rows, HEAD_SIZE), f32),
            pltpu.VMEM((CHUNKS, chips, rows, width), bf16),
            pltpu.VMEM((CHUNKS, chips, rows, width), bf16),
            pltpu.VMEM((CHUNKS, chips, rows, width), f32),
            pltpu.VMEM((CHUNKS, 3, rows, width), bf16),
            pltpu.VMEM((CHUNKS, 3, rows, width), bf16),
            dma((2 + blocks,)),
            dma((7, CHUNKS)),
            dma((7, CHUNKS)),
            dma((reach, CHUNKS)),
            dma((reach, CHUNKS)),
            dma((CHUNKS,)),
            dma((CHUNKS,)),
            dma((CHUNKS, 3)),
            dma((CHUNKS, 3)),
        ],
        compiler_params=pltpu.CompilerParams(
            collective_id=0, has_side_effects=True, vmem_limit_bytes=58 * 2**20
        ),
    )(
        tokens,
        norm_gain,
        query_key_value_weight.reshape(blocks, width, columns),
        out_weight,
        doc_ids.reshape(1, length),
        local,
        base,
    )


def solution(mesh):
    return jax.shard_map(
        functools.partial(body, dict(mesh.shape)),
        mesh=mesh,
        in_specs=(
            P("tok", ("head", "grp")),
            P(("head", "grp")),
            P(None, ("head", "grp")),
            P(("head", "grp"), None),
            P("tok"),
        ),
        out_specs=P("tok", ("head", "grp")),
        check_vma=False,
    )
```
